256 devices in a mesh: vocab: 64 (over x, y_hi, z), tensor: 4 (over y_lo, core).
Axes of the slice: x: 4, y: 4 (y_hi: 2, y_lo: 2; y = y_hi * 2 + y_lo), z: 8, core: 2. Of those that a mesh axis runs over, the one named last changes fastest.
Arguments:
- teacher_rows: bfloat16 [512, 3584], P('vocab', 'tensor'), may hold values from -200 to 200
- student_rows: bfloat16 [512, 2304], P('vocab', 'tensor'), may hold values from -200 to 200
- teacher_head: bfloat16 [3584, 131072], P(None, ('vocab', 'tensor')), may hold values from -0.5 to 0.5
- student_head: bfloat16 [2304, 131072], P(None, ('vocab', 'tensor')), may hold values from -0.5 to 0.5
Outputs:
- token_kl: float32 [512], replicated
- student_rows_grad: bfloat16 [512, 2304], P('vocab', 'tensor')
- student_head_grad: bfloat16 [2304, 131072], P(None, ('vocab', 'tensor'))
The draws below stay inside these ranges and needn't reach their ends.
All inputs are finite; a program needn't handle non-finite values.
Results may differ from the reference program's by a relative error of at most 0.019.
Values may be sent and summed in bfloat16 or wider, within the bound.
No kernel may reach another device: no remote copies, remote signals or barrier semaphores. Data moves between devices by JAX's collectives and lax.ppermute only.
A program may use at most 64 MiB of HBM per device.

```python
import math
import jax
import jax.numpy as jnp
from jax import lax

DT = 3584
DS = 2304
TOKENS = 512
VOCAB = 131072


def make_pair(key, width, salt):
    key = jax.random.fold_in(key, salt)
    key_col, key_head, key_row, key_scale, key_lift = jax.random.split(key, 5)
    position = jnp.arange(VOCAB, dtype=jnp.float32) / max(VOCAB - 1, 1)
    col_scale = jnp.exp(jax.random.uniform(key_col, (VOCAB,), jnp.float32, 0.0, math.log(10.0)))
    row_scale = jnp.exp(jax.random.uniform(key_scale, (TOKENS, 1), jnp.float32, 0.0, math.log(10.0)))
    rows = jnp.clip(jax.random.normal(key_row, (TOKENS, width), jnp.float32), -5.0, 5.0) * row_scale
    lift = jax.random.uniform(key_lift, (TOKENS,), jnp.float32, 2.8, 3.4)
    rows = rows.at[:, 0].set(lift)
    head = jnp.clip(jax.random.normal(key_head, (width, VOCAB), jnp.float32), -5.0, 5.0)
    head = head * (0.025 / math.sqrt(width)) * col_scale[None, :]
    head = head.at[0].add(0.35 * position)
    head = jnp.clip(head, -0.5, 0.5)
    head = head.astype(jnp.bfloat16).astype(jnp.float32)
    rows = jnp.clip(rows, -200.0, 200.0)
    return (head, rows)


def draw_teacher_rows(key, part):
    result = make_pair(key, DT, 1)
    return result[1].astype(jnp.bfloat16)


def draw_teacher_head(key, part):
    result = make_pair(key, DT, 1)
    return result[0].astype(jnp.bfloat16)


def draw_student_rows(key, part):
    result = make_pair(key, DS, 2)
    return result[1].astype(jnp.bfloat16)


def draw_student_head(key, part):
    result = make_pair(key, DS, 2)
    return result[0].astype(jnp.bfloat16)


def setup_inputs(seed: int = 0) -> dict:
    key_list = jax.random.split(jax.random.key(seed), 5)
    return {
        "teacher_rows": draw_teacher_rows(jax.random.fold_in(key_list[4], 71), 0),
        "student_rows": draw_student_rows(jax.random.fold_in(key_list[4], 71), 0),
        "teacher_head": draw_teacher_head(jax.random.fold_in(key_list[4], 71), 0),
        "student_head": draw_student_head(jax.random.fold_in(key_list[4], 71), 0),
    }


def reference(teacher_rows, student_rows, teacher_head, student_head):
    teach_logits = jnp.dot(teacher_rows, teacher_head, preferred_element_type=jnp.float32)
    stud_logits = jnp.dot(student_rows, student_head, preferred_element_type=jnp.float32)
    teach_peak = jnp.max(teach_logits, axis=1)
    stud_peak = jnp.max(stud_logits, axis=1)
    teach_exp = jnp.exp(teach_logits - teach_peak[:, None])
    stud_exp = jnp.exp(stud_logits - stud_peak[:, None])
    teach_total = jnp.sum(teach_exp, axis=1)
    stud_total = jnp.sum(stud_exp, axis=1)
    cross = jnp.sum(teach_exp * (teach_logits - stud_logits), axis=1)
    token_kl = cross / teach_total - teach_peak - jnp.log(teach_total) + stud_peak + jnp.log(stud_total)
    logit_grad = (stud_exp / stud_total[:, None] - teach_exp / teach_total[:, None]).astype(jnp.bfloat16)
    rows_grad = lax.dot_general(logit_grad, student_head, (((1,), (1,)), ((), ())), preferred_element_type=jnp.float32)
    head_grad = lax.dot_general(student_rows, logit_grad, (((0,), (0,)), ((), ())), preferred_element_type=jnp.float32)
    return token_kl, rows_grad.astype(jnp.bfloat16), head_grad.astype(jnp.bfloat16)
```

```python
import functools
import jax
import jax.numpy as jnp
from jax import lax
from jax.experimental import pallas as pl
from jax.experimental.pallas import tpu as pltpu
from jax.sharding import Mesh, PartitionSpec as P

F32 = jnp.float32
BF16 = jnp.bfloat16
Y = ("yh", "yl")
VMEM = pl.BlockSpec(memory_space=pltpu.VMEM)
PARAMS = pltpu.CompilerParams(vmem_limit_bytes=40 * 1024 * 1024)


def rows_of(x, y, rx, ry, nx):
    sx = lax.rem(x - rx + nx, nx)
    sy = lax.rem(y - ry + 4, 4)
    return sx * 2 + sy // 2, lax.rem(sy, 2)


def place(parts, full, tokens, nx, x_outer):
    x, c = lax.axis_index("x"), lax.axis_index("c")
    y = lax.axis_index("yh") * 2 + lax.axis_index("yl")
    outer, inner = (nx, 4) if x_outer else (4, nx)
    for half in range(2):
        core = c if half == 0 else 1 - c
        for o in range(outer):
            for i in range(inner):
                block, low = rows_of(x, y, *((o, i) if x_outer else (i, o)), nx)
                full[low * 2 + core, pl.ds(pl.multiple_of(block * tokens, tokens), tokens), :] = parts[
                    half * outer + o
                ][i]


def dot_blocks(full, head, out):
    width = full.shape[2]
    for t in range(4):
        part = jnp.dot(
            full[t], head[t * width : (t + 1) * width, :], preferred_element_type=F32
        )
        if t == 0:
            out[...] = part
        else:
            out[...] += part


def student_kernel(nx, tokens, *refs):
    parts, (head, logits, full) = refs[: 2 * nx], refs[2 * nx :]
    place(parts, full, tokens, nx, True)
    dot_blocks(full, head, logits)


def teacher_kernel(nx, tokens, peers, *refs):
    parts, (head, slog, et_ref, es_ref, stats, full) = refs[:8], refs[8:]
    place(parts, full, tokens, nx, False)
    dot_blocks(full, head, et_ref)
    tl, sl = et_ref[...], slog[...]
    tm = jnp.max(tl, axis=1, keepdims=True)
    sm = jnp.max(sl, axis=1, keepdims=True)
    et, es = jnp.exp(tl - tm), jnp.exp(sl - sm)
    et_ref[...] = et
    es_ref[...] = es
    cols = (
        tm,
        sm,
        jnp.sum(et, axis=1, keepdims=True),
        jnp.sum(es, axis=1, keepdims=True),
        jnp.sum(et * (tl - sl), axis=1, keepdims=True),
    )
    lane = lax.broadcasted_iota(jnp.int32, (tl.shape[0], 128), 1)
    wide = jnp.zeros((tl.shape[0], 128), F32)
    for k, col in enumerate(cols):
        wide = jnp.where(lane == k, col, wide)
    tall = wide.T[:8]
    for p in range(peers):
        stats[p] = tall


def merge(gathered):
    n = gathered.shape[0]
    part = [gathered[p] for p in range(n)]
    tm, sm = part[0][0:1], part[0][1:2]
    for p in range(1, n):
        tm = jnp.maximum(tm, part[p][0:1])
        sm = jnp.maximum(sm, part[p][1:2])
    tt = st = cr = jnp.zeros_like(tm)
    for p in range(n):
        tscale = jnp.exp(part[p][0:1] - tm)
        tt = tt + part[p][2:3] * tscale
        st = st + part[p][3:4] * jnp.exp(part[p][1:2] - sm)
        cr = cr + part[p][4:5] * tscale
    return tm, sm, tt, st, cr


def merge_kernel(gathered, out):
    rows = merge(gathered)
    value = jnp.concatenate(list(rows) + [jnp.zeros_like(rows[0])] * 3, axis=0)
    for p in range(out.shape[0]):
        out[p] = value


def grad_kernel(gathered, own, et, es, head, kl, grad, mine, theirs):
    tm, sm, tt, st, cr = merge(gathered)
    kl[...] = jnp.broadcast_to(cr / tt - tm - jnp.log(tt) + sm + jnp.log(st), kl.shape)
    mine_stats = own[0]
    tscale = jnp.exp(mine_stats[0:1] - tm) / tt
    sscale = jnp.exp(mine_stats[1:2] - sm) / st
    row = lax.broadcasted_iota(jnp.int32, (128, tm.shape[1]), 0)
    wide = jnp.where(row == 0, tscale, jnp.where(row == 1, sscale, 0.0)).T
    grad[...] = (es[...] * wide[:, 1:2] - et[...] * wide[:, 0:1]).astype(BF16)
    c = lax.axis_index("c")
    width = mine.shape[3]
    for low in range(2):
        for out, core in ((theirs, 1 - c), (mine, c)):
            start = pl.multiple_of((low * 2 + core) * width, width)
            value = lax.dot_general(
                grad[...],
                head[pl.ds(start, width), :],
                (((1,), (1,)), ((), ())),
                preferred_element_type=F32,
            )
            out[:, low] = value.reshape(out.shape[0], out.shape[2], width).astype(out.dtype)


def head_kernel(full, grad, out):
    width = full.shape[2]
    for t in range(4):
        out[t * width : (t + 1) * width, :] = lax.dot_general(
            full[t], grad[...], (((0,), (0,)), ((), ())), preferred_element_type=F32
        ).astype(BF16)


def call(kernel, operands, outs, scratch=(), flops=0):
    nbytes = sum(a.size * a.dtype.itemsize for a in list(operands) + list(outs))
    return pl.pallas_call(
        kernel,
        out_shape=outs,
        in_specs=[VMEM] * len(operands),
        out_specs=[VMEM] * len(outs),
        scratch_shapes=list(scratch),
        compiler_params=PARAMS,
        cost_estimate=pl.CostEstimate(flops=flops, bytes_accessed=nbytes, transcendentals=0),
    )(*operands)


def shift(value, axis, n, k):
    return lax.ppermute(value, axis, [(i, (i + k) % n) for i in range(n)])


def shards(sizes, teacher_rows, student_rows, teacher_head, student_head):
    nx, nz = sizes["x"], sizes["z"]
    peers = nx * 4
    wt, ws = teacher_rows.shape[1], student_rows.shape[1]
    rows = teacher_rows.shape[0]
    tokens, total = nz * rows, nx * 2 * nz * rows
    vocab = teacher_head.shape[1]

    both = jnp.concatenate([teacher_rows, student_rows], axis=1)
    both = lax.all_to_all(
        jnp.broadcast_to(both[None], (nz,) + both.shape), "z", 0, 0, tiled=True
    ).reshape(tokens, wt + ws)
    teach, stud = both[:, :wt], both[:, wt:]

    stud = jnp.stack([stud] + [shift(stud, Y, 4, k) for k in range(1, 4)])
    teach = jnp.stack([teach] + [shift(teach, "x", nx, k) for k in range(1, nx)])
    studs = [stud] + [shift(stud, "x", nx, k) for k in range(1, nx)]
    teaches = [teach] + [shift(teach, Y, 4, k) for k in range(1, 4)]
    studs += [shift(part, "c", 2, 1) for part in studs]
    teaches += [shift(part, "c", 2, 1) for part in teaches]

    sds = jax.ShapeDtypeStruct
    stud_logits, stud_full = call(
        functools.partial(student_kernel, nx, tokens),
        studs + [student_head],
        [sds((total, vocab), F32), sds((4, total, ws), BF16)],
        flops=8 * total * ws * vocab,
    )
    et, es, stats = call(
        functools.partial(teacher_kernel, nx, tokens, peers),
        teaches + [teacher_head, stud_logits],
        [sds((total, vocab), F32), sds((total, vocab), F32), sds((peers, 8, total), F32)],
        scratch=[pltpu.VMEM((4, total, wt), BF16)],
        flops=8 * total * wt * vocab,
    )
    gathered = lax.all_to_all(stats, ("x", "yh", "yl"), 0, 0, tiled=True)
    (gathered,) = call(merge_kernel, [gathered], [sds((nz * 2, 8, total), F32)])
    gathered = lax.all_to_all(gathered, ("z", "c"), 0, 0, tiled=True)
    kl, grad, mine, theirs = call(
        grad_kernel,
        [gathered, stats, et, es, student_head],
        [
            sds((8, total), F32),
            sds((total, vocab), BF16),
            sds((nx * 2, 2, tokens, ws), F32),
            sds((nx * 2, 2, tokens, ws), BF16),
        ],
        flops=8 * total * ws * vocab,
    )
    (head_grad,) = call(
        head_kernel,
        [stud_full, grad],
        [sds(student_head.shape, BF16)],
        flops=8 * total * ws * vocab,
    )
    part = (mine + shift(theirs, "c", 2, 1).astype(F32)).astype(BF16)
    part = lax.all_to_all(
        part.reshape(peers, tokens, ws), ("x", "yh", "yl"), 0, 0, tiled=True
    )
    part = jnp.sum(part.astype(F32), axis=0).astype(BF16)
    part = lax.all_to_all(part.reshape(nz, rows, ws), "z", 0, 0, tiled=True)
    rows_grad = jnp.sum(part.astype(F32), axis=0).astype(BF16)
    return kl[0], rows_grad, head_grad


def program(mesh):
    vocab, tensor = ("x", "yh", "z"), ("yl", "c")
    placed = (
        P(vocab, tensor),
        P(vocab, tensor),
        P(None, vocab + tensor),
        P(None, vocab + tensor),
    )
    return jax.shard_map(
        functools.partial(shards, dict(mesh.shape)),
        mesh=mesh,
        in_specs=placed,
        out_specs=(P(), P(vocab, tensor), P(None, vocab + tensor)),
        check_vma=False,
    )


def solution(mesh):
    nz = mesh.shape["vocab"] // 8
    return program(
        Mesh(mesh.devices.reshape(4, 2, nz, 2, 2), ("x", "yh", "z", "yl", "c"))
    )
```

```python
import functools
import jax
import jax.numpy as jnp
from jax import lax
from jax.experimental import pallas as pl
from jax.experimental.pallas import tpu as pltpu
from jax.sharding import Mesh, PartitionSpec as P

F32 = jnp.float32
BF16 = jnp.bfloat16
Y = ("yh", "yl")
STEPS = (0, 2, 1, 3)
FLIPS = (0, 1, 3, 2)
VMEM = pl.BlockSpec(memory_space=pltpu.VMEM)
PARAMS = pltpu.CompilerParams(vmem_limit_bytes=20 * 1024 * 1024)


def place_kernel(x_outer, *refs):
    parts, out = refs[:4], refs[4]
    tokens = parts[0].shape[1]
    x = lax.axis_index("x")
    y = lax.axis_index("yh") * 2 + lax.axis_index("yl")
    outer, inner = (x, y) if x_outer else (y, x)
    for part, step in zip(parts, STEPS):
        there = lax.rem(outer - step + 4, 4)
        for at, flip in enumerate(FLIPS):
            here = lax.bitwise_xor(inner, flip)
            sx, sy = (there, here) if x_outer else (here, there)
            block = sx * 2 + lax.div(sy, 2)
            rows = pl.ds(pl.multiple_of(block * tokens, tokens), tokens)
            out[lax.rem(sy, 2), rows, :] = part[at]


def student_kernel(extra, own, sibling, head, logits, full):
    c = lax.axis_index("c")
    width = full.shape[2]
    for low in range(2):
        full[low * 2 + c] = own[low, :, extra : extra + width]
        full[low * 2 + 1 - c] = sibling[low, :, extra : extra + width]
    for t in range(4):
        part = jnp.dot(
            full[t], head[t * width : (t + 1) * width, :], preferred_element_type=F32
        )
        if t == 0:
            logits[...] = part
        else:
            logits[...] += part


def teacher_part(columns, head, core, out, first):
    width = head.shape[0] // 4
    for low in range(2):
        start = pl.multiple_of((low * 2 + core) * width, width)
        value = jnp.dot(columns(low), head[pl.ds(start, width), :], preferred_element_type=F32)
        if first and low == 0:
            out[...] = value
        else:
            out[...] += value


def teacher_own_kernel(own, rest, head, out):
    extra = head.shape[0] // 4 - own.shape[2]

    def columns(low):
        return jnp.concatenate([own[low], rest[low, :, :extra]], axis=1)

    teacher_part(columns, head, lax.axis_index("c"), out, True)


def teacher_kernel(sibling, rest, head, begun, slog, et_ref, es_ref, stats):
    extra = head.shape[0] // 4 - sibling.shape[2]

    def columns(low):
        return jnp.concatenate([sibling[low], rest[low, :, :extra]], axis=1)

    et_ref[...] = begun[...]
    teacher_part(columns, head, 1 - lax.axis_index("c"), et_ref, False)
    tl, sl = et_ref[...], slog[...]
    tm = jnp.max(tl, axis=1, keepdims=True)
    sm = jnp.max(sl, axis=1, keepdims=True)
    et, es = jnp.exp(tl - tm), jnp.exp(sl - sm)
    et_ref[...] = et
    es_ref[...] = es
    cols = (
        tm,
        sm,
        jnp.sum(et, axis=1, keepdims=True),
        jnp.sum(es, axis=1, keepdims=True),
        jnp.sum(et * (tl - sl), axis=1, keepdims=True),
    )
    lane = lax.broadcasted_iota(jnp.int32, (tl.shape[0], 128), 1)
    wide = jnp.zeros((tl.shape[0], 128), F32)
    for k, col in enumerate(cols):
        wide = jnp.where(lane == k, col, wide)
    stats[...] = wide.T[:8]


def merge(gathered):
    n = gathered.shape[0]
    part = [gathered[p] for p in range(n)]
    tm, sm = part[0][0:1], part[0][1:2]
    for p in range(1, n):
        tm = jnp.maximum(tm, part[p][0:1])
        sm = jnp.maximum(sm, part[p][1:2])
    tt = st = cr = jnp.zeros_like(tm)
    for p in range(n):
        tscale = jnp.exp(part[p][0:1] - tm)
        tt = tt + part[p][2:3] * tscale
        st = st + part[p][3:4] * jnp.exp(part[p][1:2] - sm)
        cr = cr + part[p][4:5] * tscale
    return tm, sm, tt, st, cr


def merge_kernel(*refs):
    sources, out = refs[:-1], refs[-1]
    part = jnp.stack([r[...] for r in sources]) if len(sources) > 1 else sources[0]
    rows = merge(part)
    value = jnp.concatenate(list(rows) + [jnp.zeros_like(rows[0])] * 3, axis=0)
    for p in range(out.shape[0]):
        out[p] = value


def grad_kernel(gathered, own, et, es, head, kl, grad, theirs):
    tm, sm, tt, st, cr = merge(gathered)
    kl[...] = (cr / tt - tm - jnp.log(tt) + sm + jnp.log(st)).reshape(kl.shape)
    mine_stats = own[...]
    tscale = jnp.exp(mine_stats[0:1] - tm) / tt
    sscale = jnp.exp(mine_stats[1:2] - sm) / st
    row = lax.broadcasted_iota(jnp.int32, (128, tm.shape[1]), 0)
    wide = jnp.where(row == 0, tscale, jnp.where(row == 1, sscale, 0.0)).T
    grad[...] = (es[...] * wide[:, 1:2] - et[...] * wide[:, 0:1]).astype(BF16)
    rows_part(grad, head, 1 - lax.axis_index("c"), theirs)


def rows_part(grad, head, core, out):
    width = out.shape[3]
    for low in range(2):
        start = pl.multiple_of((low * 2 + core) * width, width)
        value = lax.dot_general(
            grad[...],
            head[pl.ds(start, width), :],
            (((1,), (1,)), ((), ())),
            preferred_element_type=F32,
        )
        out[:, low] = value.reshape(out.shape[0], out.shape[2], width).astype(out.dtype)


def mine_kernel(grad, head, mine):
    rows_part(grad, head, lax.axis_index("c"), mine)


def head_kernel(full, grad, out):
    width = full.shape[2]
    for t in range(4):
        out[t * width : (t + 1) * width, :] = lax.dot_general(
            full[t], grad[...], (((0,), (0,)), ((), ())), preferred_element_type=F32
        ).astype(BF16)


def pack_kernel(mine, theirs, out):
    half, width = out.shape[1], mine.shape[3]
    for block in range(mine.shape[0]):
        for low in range(2):
            value = (mine[block, low] + theirs[block, low].astype(F32)).astype(BF16)
            out[block * 2 + low, :, :width] = value[:half]
            out[block * 2 + low, :, width:] = value[half:]


def unpack_kernel(parts, out):
    half, width = parts.shape[1], out.shape[1]
    value = parts[0].astype(F32)
    for p in range(1, parts.shape[0]):
        value = value + parts[p].astype(F32)
    value = value.astype(BF16)
    out[:half] = value[:, :width]
    out[half:] = value[:, width:]


def call(kernel, operands, outs, scratch=(), flops=0):
    nbytes = sum(a.size * a.dtype.itemsize for a in list(operands) + list(outs))
    return pl.pallas_call(
        kernel,
        out_shape=outs,
        in_specs=[VMEM] * len(operands),
        out_specs=[VMEM] * len(outs),
        scratch_shapes=list(scratch),
        compiler_params=PARAMS,
        cost_estimate=pl.CostEstimate(flops=flops, bytes_accessed=nbytes, transcendentals=0),
    )(*operands)


def shift(value, axis, n, k):
    return lax.ppermute(value, axis, [(i, (i + k) % n) for i in range(n)])


def flip(value, axis, k):
    return lax.ppermute(value, axis, [(i, i ^ k) for i in range(4)])


def shards(sizes, teacher_rows, student_rows, teacher_head, student_head):
    nz = sizes["z"]
    wt, ws = teacher_rows.shape[1], student_rows.shape[1]
    rows = teacher_rows.shape[0]
    tokens, total = nz * rows, 8 * nz * rows
    vocab = teacher_head.shape[1]
    cut = (wt + ws) // 256 * 128 + 128

    fill = -(wt + ws) % 128
    both = jnp.concatenate(
        [teacher_rows, student_rows, jnp.zeros((rows, fill), BF16)], axis=1
    )
    both = lax.all_to_all(
        jnp.broadcast_to(both[None], (nz,) + both.shape), "z", 0, 0, tiled=True
    ).reshape(1, tokens, wt + ws + fill)
    a, b = both[:, :, :cut], both[:, :, cut:]
    for k in (1, 3):
        more = flip(a, "x", k), flip(b, Y, k)
        a, b = jnp.concatenate([a, more[0]]), jnp.concatenate([b, more[1]])
        a, b = lax.optimization_barrier((a, b))
    a_1, a_3 = shift(a, Y, 4, 1), shift(a, Y, 4, 3)
    b_1, b_3, b_2 = (shift(b, "x", 4, k) for k in (1, 3, 2))
    late, b_1, b_3 = lax.optimization_barrier((a, b_1, b_3))
    a_parts, b_parts = [a, shift(late, Y, 4, 2), a_1, a_3], [b, b_2, b_1, b_3]

    sds = jax.ShapeDtypeStruct
    (b_own,) = call(
        functools.partial(place_kernel, True), b_parts, [sds((2, total, wt + ws + fill - cut), BF16)]
    )
    b_sib = shift(b_own, "c", 2, 1)
    (a_own,) = call(functools.partial(place_kernel, False), a_parts, [sds((2, total, cut), BF16)])
    a_sib = shift(a_own, "c", 2, 1)
    stud_logits, stud_full = call(
        functools.partial(student_kernel, wt - cut),
        [b_own, b_sib, student_head],
        [sds((total, vocab), F32), sds((4, total, ws), BF16)],
        flops=8 * total * ws * vocab,
    )
    (teach_part,) = call(
        teacher_own_kernel,
        [a_own, b_own, teacher_head],
        [sds((total, vocab), F32)],
        flops=4 * total * wt * vocab,
    )
    et, es, stats = call(
        teacher_kernel,
        [a_sib, b_sib, teacher_head, teach_part, stud_logits],
        [sds((total, vocab), F32), sds((total, vocab), F32), sds((8, total), F32)],
        flops=4 * total * wt * vocab,
    )
    (gathered,) = call(
        merge_kernel, [stats, shift(stats, "c", 2, 1)], [sds((16, 8, total), F32)]
    )
    gathered = lax.all_to_all(gathered, ("x", "yh", "yl"), 0, 0, tiled=True)
    (gathered,) = call(merge_kernel, [gathered], [sds((nz, 8, total), F32)])
    gathered = lax.all_to_all(gathered, "z", 0, 0, tiled=True)
    kl, grad, theirs = call(
        grad_kernel,
        [gathered, stats, et, es, student_head],
        [sds((total,), F32), sds((total, vocab), BF16), sds((8, 2, tokens, ws), BF16)],
        flops=4 * total * ws * vocab,
    )
    theirs = shift(theirs, "c", 2, 1)
    (mine,) = call(
        mine_kernel,
        [grad, student_head],
        [sds((8, 2, tokens, ws), F32)],
        flops=4 * total * ws * vocab,
    )
    (part,) = call(pack_kernel, [mine, theirs], [sds((16, tokens // 2, 2 * ws), BF16)])
    part = lax.all_to_all(part, ("x", "yh", "yl"), 0, 0, tiled=True)
    (part,) = call(unpack_kernel, [part], [sds((tokens, ws), BF16)])
    part, grad = lax.optimization_barrier((part, grad))
    (head_grad,) = call(
        head_kernel,
        [stud_full, grad],
        [sds(student_head.shape, BF16)],
        flops=8 * total * ws * vocab,
    )
    part = lax.all_to_all(part.reshape(nz, rows, ws), "z", 0, 0, tiled=True)
    rows_grad = jnp.sum(part.astype(F32), axis=0).astype(BF16)
    return kl, rows_grad, head_grad


def program(mesh):
    vocab, tensor = ("x", "yh", "z"), ("yl", "c")
    placed = (
        P(vocab, tensor),
        P(vocab, tensor),
        P(None, vocab + tensor),
        P(None, vocab + tensor),
    )
    return jax.shard_map(
        functools.partial(shards, dict(mesh.shape)),
        mesh=mesh,
        in_specs=placed,
        out_specs=(P(), P(vocab, tensor), P(None, vocab + tensor)),
        check_vma=False,
    )


def solution(mesh):
    nz = mesh.shape["vocab"] // 8
    return program(
        Mesh(mesh.devices.reshape(4, 2, nz, 2, 2), ("x", "yh", "z", "yl", "c"))
    )
```

```python
import functools
import jax
import jax.numpy as jnp
from jax import lax
from jax.experimental import pallas as pl
from jax.experimental.pallas import tpu as pltpu
from jax.sharding import Mesh, PartitionSpec as P

F32 = jnp.float32
BF16 = jnp.bfloat16
STEPS = (0, 2, 1, 3)
VMEM = pl.BlockSpec(memory_space=pltpu.VMEM)
HBM = pl.BlockSpec(memory_space=pltpu.HBM)
PARAMS = pltpu.CompilerParams(vmem_limit_bytes=16 * 1024 * 1024)


def place(parts, role, full):
    tokens = parts[0].shape[1]
    x = lax.axis_index("x")
    y = lax.axis_index("yh") * 2 + lax.axis_index("yl")
    for part, step in zip(parts, STEPS):
        for at, by in enumerate(STEPS):
            sx = jnp.where(role == 0, lax.rem(x - by + 4, 4), lax.rem(x - step + 4, 4))
            sy = jnp.where(role == 0, lax.rem(y - step + 4, 4), lax.rem(y - by + 4, 4))
            block = sx * 2 + lax.div(sy, 2)
            rows = pl.ds(pl.multiple_of(block * tokens, tokens), tokens)
            full[lax.rem(sy, 2), rows, :] = part[at]


def head_rows(low, core, head):
    width = head.shape[0] // 4
    return head[pl.ds(pl.multiple_of((low * 2 + core) * width, width), width), :]


def products(full, core, student, teacher, cols):
    wt, ws = teacher.shape[0] // 4, student.shape[0] // 4
    slog = tlog = None
    for low in range(2):
        cols[low] = full[low, :, wt : wt + ws]
        s = jnp.dot(cols[low], head_rows(low, core, student), preferred_element_type=F32)
        t = jnp.dot(
            full[low, :, :wt], head_rows(low, core, teacher), preferred_element_type=F32
        )
        slog, tlog = (s, t) if low == 0 else (slog + s, tlog + t)
    return slog, tlog


def stack_kernel(*refs):
    for at, part in enumerate(refs[:-1]):
        refs[-1][at] = part[...]


def fetch_kernel(student_at, teacher_at, student, teacher, sems):
    copies = [
        pltpu.make_async_copy(student_at, student, sems.at[0]),
        pltpu.make_async_copy(teacher_at, teacher, sems.at[1]),
    ]
    for copy in copies:
        copy.start()
    for copy in copies:
        copy.wait()


def own_kernel(*refs):
    parts, (student, teacher, slog, tlog, cols, full) = refs[:4], refs[4:]
    core = lax.axis_index("c")
    place(parts, core, full)
    slog[...], tlog[...] = products(full, core, student, teacher, cols)


def sibling_kernel(*refs):
    parts, (student, teacher, slog, tlog, et_ref, es_ref, stats, cols, full) = (
        refs[:4],
        refs[4:],
    )
    core = 1 - lax.axis_index("c")
    place(parts, core, full)
    sl, tl = products(full, core, student, teacher, cols)
    tl, sl = tl + tlog[...], sl + slog[...]
    tm = jnp.max(tl, axis=1, keepdims=True)
    sm = jnp.max(sl, axis=1, keepdims=True)
    et, es = jnp.exp(tl - tm), jnp.exp(sl - sm)
    et_ref[...] = et
    es_ref[...] = es
    stat_cols = (
        tm,
        sm,
        jnp.sum(et, axis=1, keepdims=True),
        jnp.sum(es, axis=1, keepdims=True),
        jnp.sum(et * (tl - sl), axis=1, keepdims=True),
    )
    lane = lax.broadcasted_iota(jnp.int32, (tl.shape[0], 128), 1)
    wide = jnp.zeros((tl.shape[0], 128), F32)
    for k, col in enumerate(stat_cols):
        wide = jnp.where(lane == k, col, wide)
    stats[...] = wide.T[:8]


def merge(gathered):
    n = gathered.shape[0]
    part = [gathered[p] for p in range(n)]
    tm, sm = part[0][0:1], part[0][1:2]
    for p in range(1, n):
        tm = jnp.maximum(tm, part[p][0:1])
        sm = jnp.maximum(sm, part[p][1:2])
    tt = st = cr = jnp.zeros_like(tm)
    for p in range(n):
        tscale = jnp.exp(part[p][0:1] - tm)
        tt = tt + part[p][2:3] * tscale
        st = st + part[p][3:4] * jnp.exp(part[p][1:2] - sm)
        cr = cr + part[p][4:5] * tscale
    return tm, sm, tt, st, cr


def merge_kernel(*refs):
    sources, out = refs[:-1], refs[-1]
    part = jnp.stack([r[...] for r in sources]) if len(sources) > 1 else sources[0]
    rows = merge(part)
    value = jnp.concatenate(list(rows) + [jnp.zeros_like(rows[0])] * 3, axis=0)
    for p in range(out.shape[0]):
        out[p] = value


def grad_kernel(gathered, own, et, es, head, kl, grad, theirs):
    tm, sm, tt, st, cr = merge(gathered)
    kl[...] = (cr / tt - tm - jnp.log(tt) + sm + jnp.log(st)).reshape(kl.shape)
    mine_stats = own[...]
    tscale = jnp.exp(mine_stats[0:1] - tm) / tt
    sscale = jnp.exp(mine_stats[1:2] - sm) / st
    row = lax.broadcasted_iota(jnp.int32, (128, tm.shape[1]), 0)
    wide = jnp.where(row == 0, tscale, jnp.where(row == 1, sscale, 0.0)).T
    grad[...] = (es[...] * wide[:, 1:2] - et[...] * wide[:, 0:1]).astype(BF16)
    rows_part(grad, head, 1 - lax.axis_index("c"), theirs)


def rows_part(grad, head, core, out):
    width = out.shape[3]
    for low in range(2):
        start = pl.multiple_of((low * 2 + core) * width, width)
        value = lax.dot_general(
            grad[...],
            head[pl.ds(start, width), :],
            (((1,), (1,)), ((), ())),
            preferred_element_type=F32,
        )
        out[:, low] = value.reshape(out.shape[0], out.shape[2], width).astype(out.dtype)


def mine_kernel(grad, head, mine):
    rows_part(grad, head, lax.axis_index("c"), mine)


def head_kernel(own, sibling, grad, out):
    c = lax.axis_index("c")
    width = own.shape[2]
    for low in range(2):
        for cols, core in ((own, c), (sibling, 1 - c)):
            start = pl.multiple_of((low * 2 + core) * width, width)
            out[pl.ds(start, width), :] = lax.dot_general(
                cols[low], grad[...], (((0,), (0,)), ((), ())), preferred_element_type=F32
            ).astype(BF16)


def split_kernel(mine, theirs, *outs):
    c, x = lax.axis_index("c"), lax.axis_index("x")
    y = lax.axis_index("yh") * 2 + lax.axis_index("yl")
    half, width = outs[0].shape[1], mine.shape[3]
    for k in range(4):
        for other in range(4):
            to_x = jnp.where(c == 0, lax.rem(x + k, 4), other)
            to_y = jnp.where(c == 0, other, lax.rem(y + k, 4))
            block, low = to_x * 2 + lax.div(to_y, 2), lax.rem(to_y, 2)
            value = mine[block, low] + theirs[block, low].astype(F32)
            value = value.astype(outs[k].dtype)
            outs[k][other, :, :width] = value[:half]
            outs[k][other, :, width:] = value[half:]


def step_kernel(*refs):
    parts, outs = refs[:4], refs[4:]
    y = lax.axis_index("yh") * 2 + lax.axis_index("yl")
    here = jnp.where(lax.axis_index("c") == 0, y, lax.axis_index("x"))
    for k in range(4):
        at = lax.rem(here + k, 4)
        value = parts[0][at]
        for part in parts[1:]:
            value = value + part[at].astype(F32)
        outs[k][...] = value.astype(outs[k].dtype)


def last_kernel(*refs):
    parts, out = refs[:4], refs[4]
    half, width = parts[0].shape[0], out.shape[1]
    value = parts[0][...]
    for part in parts[1:]:
        value = value + part[...].astype(F32)
    value = value.astype(BF16)
    out[:half] = value[:, :width]
    out[half:] = value[:, width:]


def call(kernel, operands, outs, scratch=(), flops=0, hbm_in=0):
    nbytes = sum(a.size * a.dtype.itemsize for a in list(operands) + list(outs))
    return pl.pallas_call(
        kernel,
        out_shape=outs,
        in_specs=[HBM] * hbm_in + [VMEM] * (len(operands) - hbm_in),
        out_specs=[VMEM] * len(outs),
        scratch_shapes=list(scratch),
        compiler_params=PARAMS,
        cost_estimate=pl.CostEstimate(flops=flops, bytes_accessed=nbytes, transcendentals=0),
    )(*operands)


def swap(value):
    return lax.ppermute(value, "c", [(0, 1), (1, 0)])


def both_ways(value, move, x_core):
    pairs = []
    for x in range(4):
        for y in range(4):
            for c in range(2):
                to = (move(x), y) if c == x_core else (x, move(y))
                pairs.append(((x * 4 + y) * 2 + c, (to[0] * 4 + to[1]) * 2 + c))
    return lax.ppermute(value, ("x", "yh", "yl", "c"), pairs)


def shift(value, k, x_core):
    return both_ways(value, lambda i: (i + k) % 4, x_core)


def shards(sizes, teacher_rows, student_rows, teacher_head, student_head):
    nz = sizes["z"]
    wt, ws = teacher_rows.shape[1], student_rows.shape[1]
    rows = teacher_rows.shape[0]
    tokens, total = nz * rows, 8 * nz * rows
    vocab = teacher_head.shape[1]
    fill = -(wt + ws) % 128

    both = jnp.concatenate(
        [teacher_rows, student_rows, jnp.zeros((rows, fill), BF16)], axis=1
    )
    part = lax.all_to_all(
        jnp.broadcast_to(both[None], (nz,) + both.shape), "z", 0, 0, tiled=True
    ).reshape(tokens, wt + ws + fill)
    (part,) = call(
        stack_kernel,
        [part] + [shift(part, k, 0) for k in STEPS[1:]],
        [jax.ShapeDtypeStruct((4, tokens, wt + ws + fill), BF16)],
    )
    part, student_late, teacher_late = lax.optimization_barrier(
        (part, student_head, teacher_head)
    )
    parts = [part] + [shift(part, k, 1) for k in STEPS[1:]]
    sds = jax.ShapeDtypeStruct
    logits, cols = sds((total, vocab), F32), sds((2, total, ws), BF16)
    scratch = [pltpu.VMEM((2, total, wt + ws + fill), BF16)]
    heads = call(
        fetch_kernel,
        [student_late, teacher_late],
        [sds(student_head.shape, BF16), sds(teacher_head.shape, BF16)],
        scratch=[pltpu.SemaphoreType.DMA((2,))],
        hbm_in=2,
    )
    first, heads = lax.optimization_barrier((parts[3], heads))
    there = [swap(p) for p in parts[:3] + [first]]
    slog, tlog, stud_own = call(
        own_kernel,
        parts + list(heads),
        [logits, logits, cols],
        scratch=scratch,
        flops=4 * total * (wt + ws) * vocab,
    )
    et, es, stats, stud_sib = call(
        sibling_kernel,
        there + list(heads) + [slog, tlog],
        [logits, logits, sds((8, total), F32), cols],
        scratch=scratch,
        flops=4 * total * (wt + ws) * vocab,
    )
    (gathered,) = call(
        merge_kernel, [stats, swap(stats)], [sds((16, 8, total), F32)]
    )
    gathered = lax.all_to_all(gathered, ("x", "yh", "yl"), 0, 0, tiled=True)
    (gathered,) = call(merge_kernel, [gathered], [sds((nz, 8, total), F32)])
    gathered = lax.all_to_all(gathered, "z", 0, 0, tiled=True)
    kl, grad, theirs = call(
        grad_kernel,
        [gathered, stats, et, es, student_head],
        [sds((total,), F32), sds((total, vocab), BF16), sds((8, 2, tokens, ws), BF16)],
        flops=4 * total * ws * vocab,
    )
    theirs = swap(theirs)
    (mine,) = call(
        mine_kernel,
        [grad, student_head],
        [sds((8, 2, tokens, ws), F32)],
        flops=4 * total * ws * vocab,
    )
    slots = [sds((4, tokens // 2, 2 * ws), F32 if k == 0 else BF16) for k in range(4)]
    parts = call(split_kernel, [mine, theirs], slots)
    parts = [parts[0]] + [shift(parts[k], k, 0) for k in (1, 2, 3)]
    slots = [sds((tokens // 2, 2 * ws), F32 if k == 0 else BF16) for k in range(4)]
    parts = call(step_kernel, parts, slots)
    parts = [parts[0]] + [shift(parts[k], k, 1) for k in (1, 2, 3)]
    (part,) = call(last_kernel, parts, [sds((tokens, ws), BF16)])
    part, grad = lax.optimization_barrier((part, grad))
    (head_grad,) = call(
        head_kernel,
        [stud_own, stud_sib, grad],
        [sds(student_head.shape, BF16)],
        flops=8 * total * ws * vocab,
    )
    part = lax.all_to_all(part.reshape(nz, rows, ws), "z", 0, 0, tiled=True)
    rows_grad = jnp.sum(part.astype(F32), axis=0).astype(BF16)
    return kl, rows_grad, head_grad


def program(mesh):
    vocab, tensor = ("x", "yh", "z"), ("yl", "c")
    placed = (
        P(vocab, tensor),
        P(vocab, tensor),
        P(None, vocab + tensor),
        P(None, vocab + tensor),
    )
    return jax.shard_map(
        functools.partial(shards, dict(mesh.shape)),
        mesh=mesh,
        in_specs=placed,
        out_specs=(P(), P(vocab, tensor), P(None, vocab + tensor)),
        check_vma=False,
    )


def solution(mesh):
    nz = mesh.shape["vocab"] // 8
    return program(
        Mesh(mesh.devices.reshape(4, 2, nz, 2, 2), ("x", "yh", "z", "yl", "c"))
    )
```

```python
import functools
import jax
import jax.numpy as jnp
from jax import lax
from jax.experimental import pallas as pl
from jax.experimental.pallas import tpu as pltpu
from jax.sharding import Mesh, PartitionSpec as P

F32 = jnp.float32
BF16 = jnp.bfloat16
STEPS = (0, 2, 1, 3)
VMEM = pl.BlockSpec(memory_space=pltpu.VMEM)
HBM = pl.BlockSpec(memory_space=pltpu.HBM)
PARAMS = pltpu.CompilerParams(vmem_limit_bytes=16 * 1024 * 1024)


def place(parts, role, full):
    tokens = parts[0].shape[1]
    x = lax.axis_index("x")
    y = lax.axis_index("yh") * 2 + lax.axis_index("yl")
    for part, step in zip(parts, STEPS):
        for at, by in enumerate(STEPS):
            sx = jnp.where(role == 0, lax.rem(x - by + 4, 4), lax.rem(x - step + 4, 4))
            sy = jnp.where(role == 0, lax.rem(y - step + 4, 4), lax.rem(y - by + 4, 4))
            block = sx * 2 + lax.div(sy, 2)
            rows = pl.ds(pl.multiple_of(block * tokens, tokens), tokens)
            full[lax.rem(sy, 2), rows, :] = part[at]


def head_rows(low, core, head):
    width = head.shape[0] // 4
    return head[pl.ds(pl.multiple_of((low * 2 + core) * width, width), width), :]


def products(full, core, student, teacher, cols):
    wt, ws = teacher.shape[0] // 4, student.shape[0] // 4
    slog = tlog = None
    for low in range(2):
        cols[low] = full[low, :, wt : wt + ws]
        s = jnp.dot(cols[low], head_rows(low, core, student), preferred_element_type=F32)
        t = jnp.dot(
            full[low, :, :wt], head_rows(low, core, teacher), preferred_element_type=F32
        )
        slog, tlog = (s, t) if low == 0 else (slog + s, tlog + t)
    return slog, tlog


def stack_kernel(*refs):
    for at, part in enumerate(refs[:-1]):
        refs[-1][at] = part[...]


def fetch_kernel(student_at, teacher_at, student, teacher, sems):
    copies = [
        pltpu.make_async_copy(student_at, student, sems.at[0]),
        pltpu.make_async_copy(teacher_at, teacher, sems.at[1]),
    ]
    for copy in copies:
        copy.start()
    for copy in copies:
        copy.wait()


def own_kernel(*refs):
    parts, (student, teacher, slog, tlog, cols, full) = refs[:4], refs[4:]
    core = lax.axis_index("c")
    place(parts, core, full)
    slog[...], tlog[...] = products(full, core, student, teacher, cols)


def sibling_kernel(*refs):
    parts, (student, teacher, slog, tlog, et_ref, es_ref, stats, cols, full) = (
        refs[:4],
        refs[4:],
    )
    core = 1 - lax.axis_index("c")
    place(parts, core, full)
    sl, tl = products(full, core, student, teacher, cols)
    tl, sl = tl + tlog[...], sl + slog[...]
    tm = jnp.max(tl, axis=1, keepdims=True)
    sm = jnp.max(sl, axis=1, keepdims=True)
    et, es = jnp.exp(tl - tm), jnp.exp(sl - sm)
    et_ref[...] = et
    es_ref[...] = es
    stat_cols = (
        tm,
        sm,
        jnp.sum(et, axis=1, keepdims=True),
        jnp.sum(es, axis=1, keepdims=True),
        jnp.sum(et * (tl - sl), axis=1, keepdims=True),
    )
    lane = lax.broadcasted_iota(jnp.int32, (tl.shape[0], 128), 1)
    wide = jnp.zeros((tl.shape[0], 128), F32)
    for k, col in enumerate(stat_cols):
        wide = jnp.where(lane == k, col, wide)
    stats[...] = wide.T[:8]


def merge(gathered):
    n = gathered.shape[0]
    part = [gathered[p] for p in range(n)]
    tm, sm = part[0][0:1], part[0][1:2]
    for p in range(1, n):
        tm = jnp.maximum(tm, part[p][0:1])
        sm = jnp.maximum(sm, part[p][1:2])
    tt = st = cr = jnp.zeros_like(tm)
    for p in range(n):
        tscale = jnp.exp(part[p][0:1] - tm)
        tt = tt + part[p][2:3] * tscale
        st = st + part[p][3:4] * jnp.exp(part[p][1:2] - sm)
        cr = cr + part[p][4:5] * tscale
    return tm, sm, tt, st, cr


def merge_kernel(*refs):
    sources, out = refs[:-1], refs[-1]
    part = jnp.stack([r[...] for r in sources]) if len(sources) > 1 else sources[0]
    rows = merge(part)
    value = jnp.concatenate(list(rows) + [jnp.zeros_like(rows[0])] * 3, axis=0)
    for p in range(out.shape[0]):
        out[p] = value


def grad_kernel(gathered, own, et, es, head, kl, grad, theirs):
    tm, sm, tt, st, cr = merge(gathered)
    kl[...] = (cr / tt - tm - jnp.log(tt) + sm + jnp.log(st)).reshape(kl.shape)
    mine_stats = own[...]
    tscale = jnp.exp(mine_stats[0:1] - tm) / tt
    sscale = jnp.exp(mine_stats[1:2] - sm) / st
    row = lax.broadcasted_iota(jnp.int32, (128, tm.shape[1]), 0)
    wide = jnp.where(row == 0, tscale, jnp.where(row == 1, sscale, 0.0)).T
    grad[...] = (es[...] * wide[:, 1:2] - et[...] * wide[:, 0:1]).astype(BF16)
    rows_part(grad, head, 1 - lax.axis_index("c"), theirs)


def rows_part(grad, head, core, out):
    width = out.shape[3]
    for low in range(2):
        start = pl.multiple_of((low * 2 + core) * width, width)
        value = lax.dot_general(
            grad[...],
            head[pl.ds(start, width), :],
            (((1,), (1,)), ((), ())),
            preferred_element_type=F32,
        )
        out[:, low] = value.reshape(out.shape[0], out.shape[2], width).astype(out.dtype)


def mine_kernel(grad, head, mine):
    rows_part(grad, head, lax.axis_index("c"), mine)


def head_kernel(own, sibling, grad, out):
    c = lax.axis_index("c")
    width = own.shape[2]
    for low in range(2):
        for cols, core in ((own, c), (sibling, 1 - c)):
            start = pl.multiple_of((low * 2 + core) * width, width)
            out[pl.ds(start, width), :] = lax.dot_general(
                cols[low], grad[...], (((0,), (0,)), ((), ())), preferred_element_type=F32
            ).astype(BF16)


def split_kernel(mine, theirs, *outs):
    c, x = lax.axis_index("c"), lax.axis_index("x")
    y = lax.axis_index("yh") * 2 + lax.axis_index("yl")
    half, width = outs[0].shape[1], mine.shape[3]
    for k in range(4):
        for other in range(4):
            to_x = jnp.where(c == 0, lax.rem(x + k, 4), other)
            to_y = jnp.where(c == 0, other, lax.rem(y + k, 4))
            block, low = to_x * 2 + lax.div(to_y, 2), lax.rem(to_y, 2)
            value = mine[block, low] + theirs[block, low].astype(F32)
            value = value.astype(outs[k].dtype)
            outs[k][other, :, :width] = value[:half]
            outs[k][other, :, width:] = value[half:]


def step_kernel(*refs):
    parts, outs = refs[:4], refs[4:]
    y = lax.axis_index("yh") * 2 + lax.axis_index("yl")
    here = jnp.where(lax.axis_index("c") == 0, y, lax.axis_index("x"))
    for k in range(4):
        at = lax.rem(here + k, 4)
        value = parts[0][at]
        for part in parts[1:]:
            value = value + part[at].astype(F32)
        outs[k][...] = value.astype(outs[k].dtype)


def last_kernel(*refs):
    parts, out = refs[:4], refs[4]
    half, width = parts[0].shape[0], out.shape[1]
    value = parts[0][...]
    for part in parts[1:]:
        value = value + part[...].astype(F32)
    value = value.astype(BF16)
    out[:half] = value[:, :width]
    out[half:] = value[:, width:]


def call(kernel, operands, outs, scratch=(), flops=0, hbm_in=0):
    nbytes = sum(a.size * a.dtype.itemsize for a in list(operands) + list(outs))
    return pl.pallas_call(
        kernel,
        out_shape=outs,
        in_specs=[HBM] * hbm_in + [VMEM] * (len(operands) - hbm_in),
        out_specs=[VMEM] * len(outs),
        scratch_shapes=list(scratch),
        compiler_params=PARAMS,
        cost_estimate=pl.CostEstimate(flops=flops, bytes_accessed=nbytes, transcendentals=0),
    )(*operands)


def swap(value):
    return lax.ppermute(value, "c", [(0, 1), (1, 0)])


def both_ways(value, move, x_core):
    pairs = []
    for x in range(4):
        for y in range(4):
            for c in range(2):
                to = (move(x), y) if c == x_core else (x, move(y))
                pairs.append(((x * 4 + y) * 2 + c, (to[0] * 4 + to[1]) * 2 + c))
    return lax.ppermute(value, ("x", "yh", "yl", "c"), pairs)


def shift(value, k, x_core):
    return both_ways(value, lambda i: (i + k) % 4, x_core)


def shards(sizes, teacher_rows, student_rows, teacher_head, student_head):
    nz = sizes["z"]
    wt, ws = teacher_rows.shape[1], student_rows.shape[1]
    rows = teacher_rows.shape[0]
    tokens, total = nz * rows, 8 * nz * rows
    vocab = teacher_head.shape[1]
    fill = -(wt + ws) % 128

    both = jnp.concatenate(
        [teacher_rows, student_rows, jnp.zeros((rows, fill), BF16)], axis=1
    )
    part = lax.all_to_all(
        jnp.broadcast_to(both[None], (nz,) + both.shape), "z", 0, 0, tiled=True
    ).reshape(tokens, wt + ws + fill)
    (part,) = call(
        stack_kernel,
        [part] + [shift(part, k, 0) for k in STEPS[1:]],
        [jax.ShapeDtypeStruct((4, tokens, wt + ws + fill), BF16)],
    )
    part, student_late, teacher_late = lax.optimization_barrier(
        (part, student_head, teacher_head)
    )
    parts = [part] + [shift(part, k, 1) for k in STEPS[1:]]
    sds = jax.ShapeDtypeStruct
    logits, cols = sds((total, vocab), F32), sds((2, total, ws), BF16)
    scratch = [pltpu.VMEM((2, total, wt + ws + fill), BF16)]
    heads = call(
        fetch_kernel,
        [student_late, teacher_late],
        [sds(student_head.shape, BF16), sds(teacher_head.shape, BF16)],
        scratch=[pltpu.SemaphoreType.DMA((2,))],
        hbm_in=2,
    )
    first, heads = lax.optimization_barrier((parts[3], heads))
    there = [swap(p) for p in parts[:3] + [first]]
    slog, tlog, stud_own = call(
        own_kernel,
        parts + list(heads),
        [logits, logits, cols],
        scratch=scratch,
        flops=4 * total * (wt + ws) * vocab,
    )
    et, es, stats, stud_sib = call(
        sibling_kernel,
        there + list(heads) + [slog, tlog],
        [logits, logits, sds((8, total), F32), cols],
        scratch=scratch,
        flops=4 * total * (wt + ws) * vocab,
    )
    (gathered,) = call(
        merge_kernel, [stats, swap(stats)], [sds((16, 8, total), F32)]
    )
    gathered = lax.all_to_all(gathered, ("x", "yh", "yl"), 0, 0, tiled=True)
    (gathered,) = call(merge_kernel, [gathered], [sds((nz, 8, total), F32)])
    gathered = lax.all_to_all(gathered, "z", 0, 0, tiled=True)
    kl, grad, theirs = call(
        grad_kernel,
        [gathered, stats, et, es, student_head],
        [sds((total,), F32), sds((total, vocab), BF16), sds((8, 2, tokens, ws), BF16)],
        flops=4 * total * ws * vocab,
    )
    theirs = swap(theirs)
    (mine,) = call(
        mine_kernel,
        [grad, student_head],
        [sds((8, 2, tokens, ws), F32)],
        flops=4 * total * ws * vocab,
    )
    slots = [sds((4, tokens // 2, 2 * ws), F32 if k == 0 else BF16) for k in range(4)]
    parts = call(split_kernel, [mine, theirs], slots)
    parts = [parts[0]] + [shift(parts[k], k, 0) for k in (1, 2, 3)]
    (head_grad,) = call(
        head_kernel,
        [stud_own, stud_sib, grad],
        [sds(student_head.shape, BF16)],
        flops=8 * total * ws * vocab,
    )
    last, head_grad = lax.optimization_barrier((parts[3], head_grad))
    parts = parts[:3] + [last]
    slots = [sds((tokens // 2, 2 * ws), F32 if k == 0 else BF16) for k in range(4)]
    parts = call(step_kernel, parts, slots)
    parts = [parts[0]] + [shift(parts[k], k, 1) for k in (1, 2, 3)]
    (part,) = call(last_kernel, parts, [sds((tokens, ws), BF16)])
    part = lax.all_to_all(part.reshape(nz, rows, ws), "z", 0, 0, tiled=True)
    rows_grad = jnp.sum(part.astype(F32), axis=0).astype(BF16)
    return kl, rows_grad, head_grad


def program(mesh):
    vocab, tensor = ("x", "yh", "z"), ("yl", "c")
    placed = (
        P(vocab, tensor),
        P(vocab, tensor),
        P(None, vocab + tensor),
        P(None, vocab + tensor),
    )
    return jax.shard_map(
        functools.partial(shards, dict(mesh.shape)),
        mesh=mesh,
        in_specs=placed,
        out_specs=(P(), P(vocab, tensor), P(None, vocab + tensor)),
        check_vma=False,
    )


def solution(mesh):
    nz = mesh.shape["vocab"] // 8
    return program(
        Mesh(mesh.devices.reshape(4, 2, nz, 2, 2), ("x", "yh", "z", "yl", "c"))
    )
```
